512 devices in a mesh: dom: 128 (over z, y, core), cache: 4 (over x).
Axes of the slice: x: 4, y: 8, z: 8, core: 2. Of those that a mesh axis runs over, the one named last changes fastest.
Arguments:
- node_feats: bfloat16 [65536, 512], P('dom', 'cache'), may hold values from -6 to 6
- part_blocks: int32 [128], P('dom'), may hold values from 1 to 2, as said below
- send_rows: int32 [128, 128, 12], P('dom'), may hold values from 0 to 511, as said below
- tile_dst: int32 [128, 14], P('dom'), may hold values from -1 to 1, as said below
- tile_src: int32 [128, 14], P('dom'), may hold values from 0 to 7, as said below
- tile_mats: bfloat16 [128, 14, 256, 256], P('dom'), may hold values from -0.19921875 to 0.19921875
- history: bfloat16 [196608, 512], P(('dom', 'cache')), may hold values from -6 to 6
- self_one: bfloat16 [512, 512], P(None, 'cache'), may hold values from -0.25 to 0.25
- neigh_one: bfloat16 [512, 512], P(None, 'cache'), may hold values from -0.25 to 0.25
- bias_one: float32 [512], P('cache'), may hold values from -3 to 3
- self_two: bfloat16 [512, 512], P(None, 'cache'), may hold values from -0.25 to 0.25
- neigh_two: bfloat16 [512, 512], P(None, 'cache'), may hold values from -0.25 to 0.25
- bias_two: float32 [512], P('cache'), may hold values from -3 to 3
Outputs:
- embed: bfloat16 [65536, 512], P('dom', 'cache')
The draws below stay inside these ranges and needn't reach their ends.
Inputs may be any that keep to these rules, and one draw needn't show every extreme that they name: `part_blocks`: some partition uses all 2 blocks and some uses one. `send_rows`: entries name node slots in the sender's used blocks: below part_blocks of the sender times 256. `tile_dst`: tiles 4 b to 4 b + 3 have destination b when b is a used block, -1 otherwise; the last 6 tiles have used destinations. `tile_src`: sources below 2 are used blocks of the partition, apart from unused tiles; tile 4 * 2 + j reads halo block j.
All inputs are finite; a program needn't handle non-finite values.
Results may differ from the reference program's by a relative error of at most 0.013.
Values may be sent and summed in bfloat16 or wider, within the bound.
No kernel may reach another device: no remote copies, remote signals or barrier semaphores. Data moves between devices by JAX's collectives and lax.ppermute only.
A program may use at most 64 MiB of HBM per device.

```python
import jax
import jax.numpy as jnp
from jax import lax

F = 512
H = 512
BLK = 256
LB = 2
HBLK = 6
ROWS = 512
HROWS = 1536
SLOT = 12
NT = 14
NODES = 65536
N_DOM = 128


def blocks_of(key):
    key_a, key_b, key_c = jax.random.split(jax.random.fold_in(key, 11), 3)
    first = jax.random.randint(key_a, (N_DOM,), 1, LB + 1)
    second = jax.random.randint(key_b, (N_DOM,), 1, LB + 1)
    counts = jnp.minimum(first, second)
    chosen = jax.random.randint(key_c, (), 0, N_DOM)
    counts = counts.at[chosen].set(LB)
    counts = counts.at[(chosen + N_DOM // 2) % N_DOM].set(1)
    return (counts.astype(jnp.int32), chosen)


def tile_lists(key):
    counts, chosen = blocks_of(key)
    key_l, key_h = jax.random.split(jax.random.fold_in(key, 23), 2)
    slots = jnp.arange(4 * LB, dtype=jnp.int32)
    block_id = slots // 4
    kind = slots % 4
    local_dst = jnp.where(block_id[None, :] < counts[:, None], block_id[None, :], -1)
    picks = jax.random.randint(key_l, (N_DOM, 4 * LB), 0, counts[:, None])
    self_src = jnp.minimum(block_id[None, :], counts[:, None] - 1)
    local_src = jnp.where(kind[None, :] == 0, self_src, picks)
    halo_dst = jax.random.randint(key_h, (N_DOM, HBLK), 0, counts[:, None])
    halo_src = jnp.broadcast_to(LB + jnp.arange(HBLK, dtype=jnp.int32)[None, :], (N_DOM, HBLK))
    dst_all = jnp.concatenate([local_dst, halo_dst], axis=1).astype(jnp.int32)
    src_all = jnp.concatenate([local_src, halo_src], axis=1).astype(jnp.int32)
    return (dst_all, src_all)


def draw_part_blocks(key, part):
    counts, chosen = blocks_of(key)
    return counts


def draw_send_rows(key, part):
    counts, chosen = blocks_of(key)
    key = jax.random.fold_in(key, 2)
    limits = counts * BLK
    picked = jax.random.randint(key, (N_DOM, N_DOM, SLOT), 0, limits[:, None, None])
    picked = picked.at[chosen, 0, 0].set(LB * BLK - 1)
    return picked.astype(jnp.int32)


def draw_tile_dst(key, part):
    dst_all, src_all = tile_lists(key)
    return dst_all


def draw_tile_src(key, part):
    dst_all, src_all = tile_lists(key)
    return src_all


def levels(stream_key, shape, pieces, smallest, largest):
    factor_of = 1.0
    for position, blocks in pieces:
        steps = jax.random.uniform(jax.random.fold_in(jax.random.fold_in(stream_key, 6), position), (blocks,), jnp.float32, smallest / len(pieces), largest / len(pieces))
        factor_of = factor_of * jnp.repeat(jnp.exp(steps), shape[position] // blocks).reshape((-1,) + (1,) * (len(shape) - 1 - position))
    return factor_of


def noise(key, dims, deviation, most, cuts=(), held_as=jnp.bfloat16):
    factor_of = levels(key, dims, cuts, -0.22, 0.18) if cuts else 1.0
    array = jax.random.normal(key, dims, jnp.float32) * deviation * factor_of
    return jnp.minimum(jnp.maximum(array, -most), most).astype(held_as)


def setup_inputs(seed: int = 0) -> dict:
    arg_keys = jax.random.split(jax.random.key(seed), 14)
    node_feats = noise(arg_keys[0], (NODES, F), 1.0, 6.0, ((0, 128), (1, 4)))
    part_blocks = draw_part_blocks(jax.random.fold_in(arg_keys[13], 71), 0)
    send_rows = draw_send_rows(jax.random.fold_in(arg_keys[13], 71), 0)
    tile_dst = draw_tile_dst(jax.random.fold_in(arg_keys[13], 71), 0)
    tile_src = draw_tile_src(jax.random.fold_in(arg_keys[13], 71), 0)
    tile_mats = noise(arg_keys[5], (N_DOM, NT, BLK, BLK), 0.03125, 0.19921875, ((0, 128),))
    history = noise(arg_keys[6], (N_DOM * HROWS, H), 1.0, 6.0, ((0, 512),))
    self_one = noise(arg_keys[7], (F, H), F ** -0.5, 0.25, ((1, 4),))
    neigh_one = noise(arg_keys[8], (F, H), F ** -0.5, 0.25, ((1, 4),))
    bias_one = noise(arg_keys[9], (H,), 0.5, 3.0, ((0, 4),), jnp.float32)
    self_two = noise(arg_keys[10], (H, H), H ** -0.5, 0.25, ((1, 4),))
    neigh_two = noise(arg_keys[11], (H, H), H ** -0.5, 0.25, ((1, 4),))
    bias_two = noise(arg_keys[12], (H,), 0.5, 3.0, ((0, 4),), jnp.float32)
    return {"node_feats": node_feats, "part_blocks": part_blocks, "send_rows": send_rows, "tile_dst": tile_dst, "tile_src": tile_src, "tile_mats": tile_mats, "history": history, "self_one": self_one, "neigh_one": neigh_one, "bias_one": bias_one, "self_two": self_two, "neigh_two": neigh_two, "bias_two": bias_two}


epsilon = 1e-06

def aggregate(tile_mats, tile_dst, tile_src, blocks):
    gathered = jnp.take(blocks, tile_src, axis=0)
    products = jnp.einsum('tij,tjf->tif', tile_mats.astype(jnp.float32), gathered.astype(jnp.float32), precision=lax.Precision.HIGHEST)
    onehot = (tile_dst[None, :] == jnp.arange(LB, dtype=jnp.int32)[:, None]).astype(jnp.float32)
    summed = jnp.einsum('dt,tif->dif', onehot, products, precision=lax.Precision.HIGHEST)
    return summed.reshape(LB * BLK, blocks.shape[2])

def reference(node_feats, part_blocks, send_rows, tile_dst, tile_src, tile_mats, history, self_one, neigh_one, bias_one, self_two, neigh_two, bias_two):
    by_part = node_feats.reshape(N_DOM, ROWS, F)
    hist_parts = history.reshape(N_DOM, HROWS, H)
    senders = jnp.arange(N_DOM, dtype=jnp.int32)
    neigh_exact = neigh_one.astype(jnp.float32)

    def one_part(part_id):
        wanted = send_rows[:, part_id, :]
        halo_rows = by_part[senders[:, None], wanted].reshape(HBLK, BLK, F)
        own_feats = by_part[part_id]
        blocks_one = jnp.concatenate([own_feats.reshape(LB, BLK, F), halo_rows], axis=0)
        agg_one = aggregate(tile_mats[part_id], tile_dst[part_id], tile_src[part_id], blocks_one)
        pre_one = jnp.dot(own_feats, self_one, preferred_element_type=jnp.float32) + jnp.dot(agg_one, neigh_exact, precision=lax.Precision.HIGHEST) + bias_one
        hidden = jax.nn.relu(pre_one)
        mean_sq = lax.optimization_barrier(jnp.sum(hidden * hidden, axis=1, keepdims=True)) / H
        level_one = (hidden * lax.rsqrt(mean_sq + epsilon)).astype(jnp.bfloat16)
        blocks_two = jnp.concatenate([level_one.reshape(LB, BLK, H), hist_parts[part_id].reshape(HBLK, BLK, H)], axis=0)
        agg_two = aggregate(tile_mats[part_id], tile_dst[part_id], tile_src[part_id], blocks_two).astype(jnp.bfloat16)
        pre_two = jnp.dot(level_one, self_two, preferred_element_type=jnp.float32) + jnp.dot(agg_two, neigh_two, preferred_element_type=jnp.float32) + bias_two
        live_rows = jnp.arange(ROWS, dtype=jnp.int32) < part_blocks[part_id] * BLK
        return jnp.where(live_rows[:, None], pre_two, 0.0).astype(jnp.bfloat16)
    result = lax.map(one_part, senders)
    return result.reshape(NODES, H)
```

```python
import jax
import jax.numpy as jnp
from jax import lax
from jax.experimental import pallas as pl
from jax.experimental.pallas import tpu as pltpu
from jax.sharding import PartitionSpec as P

epsilon = 1e-06
VMEM = pl.BlockSpec(memory_space=pltpu.VMEM)
SMEM = pl.BlockSpec(memory_space=pltpu.SMEM)
f32, bf16 = jnp.float32, jnp.bfloat16
LB, BLK, HBLK, LOCAL, SLOT = 2, 256, 6, 8, 12
N_CACHE = 4


def call(kernel, out_shape, in_specs, scratch=(), flops=10**8, moved=10**6):
    return pl.pallas_call(
        kernel,
        out_shape=out_shape,
        in_specs=in_specs,
        out_specs=jax.tree.map(lambda _: VMEM, out_shape),
        scratch_shapes=list(scratch),
        compiler_params=pltpu.CompilerParams(vmem_limit_bytes=40 * 2**20),
        cost_estimate=pl.CostEstimate(flops=flops, bytes_accessed=moved, transcendentals=0),
    )


def mm(a, b):
    return jnp.dot(a, b, preferred_element_type=f32)


def block(ref, i):
    return ref[pl.ds(pl.multiple_of(i * BLK, BLK), BLK), :]


def gather_kernel(rows_ref, x_ref, out_ref, wide):
    dests = rows_ref.shape[1]
    rows = rows_ref[0]
    lanes = lax.broadcasted_iota(jnp.int32, (dests, x_ref.shape[0]), 1)
    x = x_ref[...]
    for s in range(SLOT):
        onehot = (lanes == rows[:, s : s + 1]).astype(f32).astype(bf16)
        wide[pl.ds(s, dests, stride=SLOT), :] = mm(onehot, x)
    out_ref[...] = wide[...].astype(bf16)


def pack_kernel(me_ref, x_ref, hist_ref, *out_refs):
    me = me_ref[0]
    rows = x_ref.shape[0]
    for d, out_ref in zip((1, 2, 3), out_refs):
        peer = lax.rem(me + d, N_CACHE)
        out_ref[:rows, :] = x_ref[...]
        out_ref[rows:, :] = hist_ref[:, pl.ds(pl.multiple_of(peer * 128, 128), 128)]


def local_sums(dst_ref, src_ref, mats_ref, pick):
    sums = []
    for b in range(LB):
        total = None
        for t in range(4 * b, 4 * b + 4):
            part = mm(mats_ref[0, t], pick(dst_ref[0, t], src_ref[0, t]))
            total = part if total is None else total + part
        sums.append(total)
    return sums


def halo_sums(dst_ref, mats_ref, halo_ref, sums):
    sums = list(sums)
    for j in range(HBLK):
        part = mm(mats_ref[0, LOCAL + j], halo_ref[j * BLK : (j + 1) * BLK, :])
        d = dst_ref[0, LOCAL + j]
        for b in range(LB):
            sums[b] = sums[b] + jnp.where(d == b, part, 0.0)
    return sums


def agg_kernel(dst_ref, src_ref, mats_ref, x_ref, halo_ref, out_ref):
    def pick(d, s):
        own = block(x_ref, jnp.minimum(s, LB - 1))
        far = block(halo_ref, jnp.maximum(s - LB, 0))
        one = jnp.where(s < LB, own, far)
        return jnp.where(d >= 0, one, jnp.zeros_like(one))

    sums = local_sums(dst_ref, src_ref, mats_ref, pick)
    sums = halo_sums(dst_ref, mats_ref, halo_ref, sums)
    for b in range(LB):
        value = sums[b].astype(bf16)
        for c in range(N_CACHE):
            out_ref[c, b * BLK : (b + 1) * BLK, :] = value


def side_kernel(
    me_ref, dst_ref, src_ref, mats_ref, x_ref, hist_ref, p1, p2, p3, w_ref, b_ref,
    self_ref, agg_ref, cols, acc,
):
    me = me_ref[0]
    rows = x_ref.shape[0]
    depth = hist_ref.shape[0]
    cols[pl.ds(pl.multiple_of(me * depth, 128), depth), :] = hist_ref[
        :, pl.ds(pl.multiple_of(me * 128, 128), 128)
    ]
    lhs, rhs = [x_ref[...]], [w_ref[pl.ds(pl.multiple_of(me * 128, 128), 128), :]]
    for d, ref in zip((1, 2, 3), (p1, p2, p3)):
        peer = lax.rem(me + N_CACHE - d, N_CACHE)
        cols[pl.ds(pl.multiple_of(peer * depth, 128), depth), :] = ref[rows:, :]
        lhs.append(ref[:rows, :])
        rhs.append(w_ref[pl.ds(pl.multiple_of(peer * 128, 128), 128), :])
    self_ref[...] = mm(jnp.concatenate(lhs, axis=1), jnp.concatenate(rhs, axis=0)) + b_ref[...]
    zero = jnp.zeros((BLK, acc.shape[1]), f32)
    sums = halo_sums(dst_ref, mats_ref, cols, [zero] * LB)
    for b in range(LB):
        acc[b * BLK : (b + 1) * BLK, :] = sums[b]
    for t in range(LOCAL):
        d, s = dst_ref[0, t], src_ref[0, t]

        @pl.when((d >= 0) & (s >= LB))
        def _():
            b = t // 4
            acc[b * BLK : (b + 1) * BLK, :] += mm(mats_ref[0, t], block(cols, s - LB))

    agg_ref[...] = acc[...].astype(bf16)


def hidden_kernel(full_ref, self_ref, w_ref, agg_ref, out_ref):
    full = jnp.concatenate([full_ref[c] for c in range(N_CACHE)], axis=1)
    rows = self_ref.shape[0]
    hidden = jnp.maximum(self_ref[...] + mm(full, w_ref[...]), 0.0).astype(bf16)
    for c in range(N_CACHE):
        out_ref[c, :rows, :] = hidden
        out_ref[c, rows:, :] = agg_ref[...]


def last_kernel(used_ref, dst_ref, src_ref, mats_ref, full_ref, ws_ref, wn_ref, b_ref, out_ref, z):
    rows = out_ref.shape[0]
    hidden = jnp.concatenate([full_ref[c, :rows, :] for c in range(N_CACHE)], axis=1)
    agg = jnp.concatenate([full_ref[c, rows:, :] for c in range(N_CACHE)], axis=1)
    wide = hidden.astype(f32)
    scale = lax.rsqrt(jnp.sum(wide * wide, axis=1, keepdims=True) / wide.shape[1] + epsilon)
    z[...] = (mm(hidden, wn_ref[...]) * scale).astype(bf16)
    base = mm(hidden, ws_ref[...]) * scale + mm(agg, wn_ref[...]) + b_ref[...]

    def pick(d, s):
        one = block(z, jnp.minimum(s, LB - 1))
        return jnp.where((d >= 0) & (s < LB), one, jnp.zeros_like(one))

    sums = local_sums(dst_ref, src_ref, mats_ref, pick)
    for b in range(LB):
        part = slice(b * BLK, (b + 1) * BLK)
        value = base[part] + sums[b]
        out_ref[part, :] = jnp.where(b < used_ref[0], value, 0.0).astype(bf16)


def body(
    x, used, send_rows, tile_dst, tile_src, mats, history,
    self_one, neigh_one, bias_one, self_two, neigh_two, bias_two,
):
    rows, width = x.shape
    depth = history.shape[0]
    dests = send_rows.shape[1]
    me = lax.axis_index("cache").astype(jnp.int32).reshape(1)
    shape = jax.ShapeDtypeStruct
    spread = dict(split_axis=0, concat_axis=0, tiled=True)

    outbound = call(
        gather_kernel, shape((dests * SLOT, width), bf16), [VMEM] * 2,
        [pltpu.VMEM((dests * SLOT, width), f32)],
    )(send_rows, x)
    halo = lax.all_to_all(outbound.reshape(dests, SLOT // 4, 4, width), "dom", **spread)
    halo = halo.reshape(dests * SLOT, width)

    packs = call(
        pack_kernel, [shape((rows + depth, width), bf16)] * 3, [SMEM, VMEM, VMEM]
    )(me, x, history)
    packs = [
        lax.ppermute(p, "cache", [(i, (i + d) % N_CACHE) for i in range(N_CACHE)])
        for d, p in zip((1, 2, 3), packs)
    ]

    agg_one = call(
        agg_kernel, shape((N_CACHE, rows, width), bf16), [SMEM] * 2 + [VMEM] * 3
    )(tile_dst, tile_src, mats, x, halo)
    agg_one = lax.all_to_all(agg_one, "cache", **spread)

    own, agg_hist = call(
        side_kernel, [shape((rows, width), f32), shape((rows, width), bf16)],
        [SMEM] * 3 + [VMEM] * 8,
        [pltpu.VMEM((HBLK * BLK, width), bf16), pltpu.VMEM((rows, width), f32)],
    )(me, tile_dst, tile_src, mats, x, history, *packs, self_one, bias_one.reshape(1, -1))

    hidden = call(
        hidden_kernel, shape((N_CACHE, 2 * rows, width), bf16), [VMEM] * 4
    )(agg_one, own, neigh_one, agg_hist)
    hidden = lax.all_to_all(hidden, "cache", **spread)

    return call(
        last_kernel, shape((rows, width), bf16), [SMEM] * 3 + [VMEM] * 5,
        [pltpu.VMEM((rows, width), bf16)],
    )(used, tile_dst, tile_src, mats, hidden, self_two, neigh_two, bias_two.reshape(1, -1))


def solution(mesh):
    return jax.shard_map(
        body,
        mesh=mesh,
        in_specs=(
            P("dom", "cache"),
            P("dom"),
            P("dom", None, None),
            P("dom", None),
            P("dom", None),
            P("dom", None, None, None),
            P(("dom", "cache"), None),
            P(None, "cache"),
            P(None, "cache"),
            P("cache"),
            P(None, "cache"),
            P(None, "cache"),
            P("cache"),
        ),
        out_specs=P("dom", "cache"),
        check_vma=False,
    )
```

```python
import jax
import jax.numpy as jnp
from jax import lax
from jax.experimental import pallas as pl
from jax.experimental.pallas import tpu as pltpu
from jax.sharding import PartitionSpec as P

epsilon = 1e-06
ANY = pl.BlockSpec(memory_space=pl.ANY)
VMEM = pl.BlockSpec(memory_space=pltpu.VMEM)
SMEM = pl.BlockSpec(memory_space=pltpu.SMEM)
f32, bf16 = jnp.float32, jnp.bfloat16
LB, BLK, HBLK, LOCAL, SLOT = 2, 256, 6, 8, 12
N_CACHE = 4


def call(kernel, out_shape, in_specs, scratch=(), out_specs=None, vmem=16):
    return pl.pallas_call(
        kernel,
        out_shape=out_shape,
        in_specs=in_specs,
        out_specs=out_specs or jax.tree.map(lambda _: VMEM, out_shape),
        scratch_shapes=list(scratch),
        compiler_params=pltpu.CompilerParams(vmem_limit_bytes=vmem * 2**20),
        cost_estimate=pl.CostEstimate(flops=2 * 10**10, bytes_accessed=10**6, transcendentals=0),
    )


def mm(a, b):
    return jnp.dot(a, b, preferred_element_type=f32)


def block(ref, i):
    return ref[pl.ds(pl.multiple_of(i * BLK, BLK), BLK), :]


def peers_of(me):
    return [me] + [lax.rem(me + N_CACHE - d, N_CACHE) for d in (1, 2, 3)]


def pack_kernel(ws_hbm, wn_hbm, x_hbm, w2_hbm, b_hbm, pack_hbm, b_ref, wide, sems):
    copies = [pltpu.make_async_copy(b_hbm, b_ref, sems.at[0])]
    copies[0].start()
    at = 0
    for k, ref in enumerate((ws_hbm, wn_hbm, x_hbm, w2_hbm)):
        part = pl.ds(at, ref.shape[0])
        copies.append(pltpu.make_async_copy(ref, wide.at[part, :], sems.at[1 + k]))
        copies[-1].start()
        at += ref.shape[0]
    copies[0].wait()
    one, parts = b_ref[...], []
    for _ in range(3):
        parts.append(one.astype(bf16))
        one = one - parts[-1].astype(f32)
    wide[at:, :] = jnp.concatenate(parts + [jnp.zeros((13, one.shape[1]), bf16)], axis=0)
    for copy in copies[1:]:
        copy.wait()
    out = pltpu.make_async_copy(wide, pack_hbm, sems.at[5])
    out.start()
    out.wait()


def gather_kernel(rows_ref, x_ref, out_ref, square, wide):
    dests = rows_ref.shape[2]
    square[...] = jnp.zeros_like(square)
    square[:SLOT, :] = rows_ref[0].astype(f32)
    rows = square[...].T.astype(jnp.int32)
    lanes = lax.broadcasted_iota(jnp.int32, (dests, x_ref.shape[0]), 1)
    x = x_ref[...]
    for s in range(SLOT):
        onehot = (lanes == rows[:, s : s + 1]).astype(f32).astype(bf16)
        wide[pl.ds(s, dests, stride=SLOT), :] = mm(onehot, x)
    out_ref[...] = wide[...].astype(bf16)


def tile_sums(dst_ref, src_ref, mats_ref, own_ref, far_ref):
    sums = []
    for b in range(LB):
        total = None
        for t in range(4 * b, 4 * b + 4):
            d, s = dst_ref[0, t], src_ref[0, t]
            own = block(own_ref, jnp.minimum(s, LB - 1))
            far = block(far_ref, jnp.maximum(s - LB, 0))
            one = jnp.where(s < LB, own, far)
            part = mm(mats_ref[0, t], jnp.where(d >= 0, one, jnp.zeros_like(one)))
            total = part if total is None else total + part
        sums.append(total)
    for j in range(HBLK):
        part = mm(mats_ref[0, LOCAL + j], far_ref[j * BLK : (j + 1) * BLK, :])
        d = dst_ref[0, LOCAL + j]
        for b in range(LB):
            sums[b] = sums[b] + jnp.where(d == b, part, 0.0)
    return sums


def agg_kernel(
    me_ref, dst_ref, src_ref, mats_ref, x_ref, halo_ref, hist_ref, n2_ref, p1, p2, p3, out_ref
):
    rows = x_ref.shape[0]
    hist = hist_ref[...]
    peers = peers_of(me_ref[0])
    out_ref[peers[0], rows:, :] = mm(hist, n2_ref[...]).astype(bf16)
    for peer, ref in zip(peers[1:], (p1, p2, p3)):
        out_ref[peer, rows:, :] = mm(hist, ref[3 * rows : 4 * rows, :]).astype(bf16)
    sums = tile_sums(dst_ref, src_ref, mats_ref, x_ref, halo_ref)
    for b in range(LB):
        value = sums[b].astype(bf16)
        for c in range(N_CACHE):
            out_ref[c, b * BLK : (b + 1) * BLK, :] = value


def last_kernel(
    me_ref, used_ref, dst_ref, src_ref, mats_ref, full_ref, x_ref, s1_ref, n1_ref, b1_ref, p1, p2, p3,
    s2_ref, n2_ref, b2_ref, out_ref, lhs, z, far,
):
    rows, width = out_ref.shape
    depth = full_ref.shape[1] - rows
    packs = (p1, p2, p3)
    cols = [pl.ds(pl.multiple_of(p * width, width), width) for p in peers_of(me_ref[0])]
    lhs[:, cols[0]] = x_ref[...]
    for ref, c in zip(packs, cols[1:]):
        lhs[:, c] = ref[2 * rows : 3 * rows, :]
    for c in range(N_CACHE):
        far[c * depth : (c + 1) * depth, :] = full_ref[c, rows:, :]
    xa = jnp.concatenate([lhs[...]] + [full_ref[c, :rows, :] for c in range(N_CACHE)], axis=1)
    first = [jnp.concatenate([s1_ref[...], n1_ref[...]], axis=0)] + [p[: 2 * rows, :] for p in packs]
    bias = [b1_ref[...]]
    for p in packs:
        terms = p[4 * rows :, :].astype(f32)
        bias.append(terms[0:1] + terms[1:2] + terms[2:3])
    hidden, squares = [], 0.0
    for i in (0, 2):
        pre = mm(xa, jnp.concatenate(first[i : i + 2], axis=1)) + jnp.concatenate(bias[i : i + 2], axis=1)
        one = jnp.maximum(pre, 0.0)
        squares = squares + jnp.sum(one * one, axis=1, keepdims=True)
        hidden.append(one.astype(bf16))
    hidden = jnp.concatenate(hidden, axis=1)
    scale = lax.rsqrt(squares / hidden.shape[1] + epsilon)
    second = jnp.concatenate(
        [jnp.concatenate([ref[c, :] for c in cols], axis=0) for ref in (s2_ref, n2_ref)], axis=1
    )
    both = mm(hidden, second) * scale
    z[...] = both[:, width:].astype(bf16)
    base = both[:, :width] + b2_ref[...]
    sums = tile_sums(dst_ref, src_ref, mats_ref, z, far)
    for b in range(LB):
        part = slice(b * BLK, (b + 1) * BLK)
        value = base[part] + sums[b]
        out_ref[part, :] = jnp.where(b < used_ref[0], value, 0.0).astype(bf16)


def body(
    x, used, send_rows, tile_dst, tile_src, mats, history,
    self_one, neigh_one, bias_one, self_two, neigh_two, bias_two,
):
    rows, width = x.shape
    depth = history.shape[0]
    dests = send_rows.shape[1]
    me = lax.axis_index("cache").astype(jnp.int32).reshape(1)
    shape = jax.ShapeDtypeStruct
    spread = dict(split_axis=0, concat_axis=0, tiled=True)
    bias = bias_one.reshape(1, -1)

    pack = call(
        pack_kernel, shape((4 * rows + 16, width), bf16), [ANY] * 5,
        [
            pltpu.VMEM((1, width), f32),
            pltpu.VMEM((4 * rows + 16, width), bf16),
            pltpu.SemaphoreType.DMA((6,)),
        ],
        out_specs=ANY, vmem=56,
    )(self_one, neigh_one, x, neigh_two, bias)
    sent = [
        lax.ppermute(pack, "cache", [(i, (i + d) % N_CACHE) for i in range(N_CACHE)]) for d in (1, 2, 3)
    ]
    outbound = call(
        gather_kernel, shape((dests * SLOT, width), bf16), [VMEM] * 2,
        [pltpu.VMEM((dests, dests), f32), pltpu.VMEM((dests * SLOT, width), f32)],
    )(jnp.swapaxes(send_rows, 1, 2), x)
    halo = lax.cond(
        used[0] > 0,
        lambda v: lax.all_to_all(v, "dom", **spread),
        jnp.zeros_like,
        outbound.reshape(dests, SLOT // 4, 4, width),
    )
    halo = halo.reshape(dests * SLOT, width)

    full = call(
        agg_kernel, shape((N_CACHE, rows + depth, width), bf16), [SMEM] * 3 + [VMEM] * 8
    )(me, tile_dst, tile_src, mats, x, halo, history, neigh_two, *sent)
    full = lax.all_to_all(full, "cache", **spread)

    return call(
        last_kernel, shape((rows, width), bf16), [SMEM] * 4 + [VMEM] * 12,
        [
            pltpu.VMEM((rows, N_CACHE * width), bf16),
            pltpu.VMEM((rows, width), bf16),
            pltpu.VMEM((HBLK * BLK, width), bf16),
        ],
    )(
        me, used, tile_dst, tile_src, mats, full, x, self_one, neigh_one, bias, *sent,
        self_two, neigh_two, bias_two.reshape(1, -1),
    )


def solution(mesh):
    return jax.shard_map(
        body,
        mesh=mesh,
        in_specs=(
            P("dom", "cache"),
            P("dom"),
            P("dom", None, None),
            P("dom", None),
            P("dom", None),
            P("dom", None, None, None),
            P(("dom", "cache"), None),
            P(None, "cache"),
            P(None, "cache"),
            P("cache"),
            P(None, "cache"),
            P(None, "cache"),
            P("cache"),
        ),
        out_specs=P("dom", "cache"),
        check_vma=False,
    )
```

```python
import jax
import jax.numpy as jnp
from jax import lax
from jax.experimental import pallas as pl
from jax.experimental.pallas import tpu as pltpu
from jax.sharding import PartitionSpec as P

epsilon = 1e-06
ANY = pl.BlockSpec(memory_space=pl.ANY)
VMEM = pl.BlockSpec(memory_space=pltpu.VMEM)
SMEM = pl.BlockSpec(memory_space=pltpu.SMEM)
f32, bf16 = jnp.float32, jnp.bfloat16
LB, BLK, HBLK, LOCAL, SLOT = 2, 256, 6, 8, 12
N_CACHE = 4


def call(kernel, out_shape, in_specs, scratch=(), out_specs=None, vmem=16, flops=2 * 10**10):
    return pl.pallas_call(
        kernel,
        out_shape=out_shape,
        in_specs=in_specs,
        out_specs=out_specs or jax.tree.map(lambda _: VMEM, out_shape),
        scratch_shapes=list(scratch),
        compiler_params=pltpu.CompilerParams(vmem_limit_bytes=vmem * 2**20),
        cost_estimate=pl.CostEstimate(flops=flops, bytes_accessed=10**6, transcendentals=0),
    )


def mm(a, b):
    return jnp.dot(a, b, preferred_element_type=f32)


def block(ref, i):
    return ref[pl.ds(pl.multiple_of(i * BLK, BLK), BLK), :]


def peers_of(me):
    return [me] + [lax.rem(me + N_CACHE - d, N_CACHE) for d in (1, 2, 3)]


def pack_kernel(ws_hbm, wn_hbm, x_hbm, hist_hbm, b_hbm, pack_hbm, b_ref, wide, sems):
    load = pltpu.make_async_copy(b_hbm, b_ref, sems.at[0])
    load.start()
    rows, width = x_hbm.shape
    parts = [(ref, k * rows) for k, ref in enumerate((ws_hbm, wn_hbm, x_hbm))]
    tail = 3 * rows
    for k in range(N_CACHE):
        parts.append((hist_hbm.at[:, pl.ds(k * width, width)], tail + 16 + k * hist_hbm.shape[0]))
    copies = []
    for k, (ref, at) in enumerate(parts):
        copies.append(pltpu.make_async_copy(ref, wide.at[pl.ds(at, ref.shape[0]), :], sems.at[1 + k]))
        copies[-1].start()
    load.wait()
    one, terms = b_ref[...], []
    for _ in range(3):
        terms.append(one.astype(bf16))
        one = one - terms[-1].astype(f32)
    wide[tail : tail + 16, :] = jnp.concatenate(terms + [jnp.zeros((13, width), bf16)], axis=0)
    for copy in copies:
        copy.wait()
    out = pltpu.make_async_copy(wide, pack_hbm, sems.at[8])
    out.start()
    out.wait()


def gather_kernel(rows_ref, x_ref, out_ref, square, wide):
    dests = rows_ref.shape[2]
    square[...] = jnp.zeros_like(square)
    square[:SLOT, :] = rows_ref[0].astype(f32)
    rows = square[...].T.astype(jnp.int32)
    lanes = lax.broadcasted_iota(jnp.int32, (dests, x_ref.shape[0]), 1)
    x = x_ref[...]
    for s in range(SLOT):
        onehot = (lanes == rows[:, s : s + 1]).astype(f32).astype(bf16)
        wide[pl.ds(s, dests, stride=SLOT), :] = mm(onehot, x)
    out_ref[...] = wide[...].astype(bf16)


def tile_sums(dst_ref, src_ref, mats_ref, own_ref, far_ref):
    sums = []
    for b in range(LB):
        tiles, ones = range(4 * b, 4 * b + 4), []
        for t in tiles:
            d, s = dst_ref[0, t], src_ref[0, t]
            own = block(own_ref, jnp.minimum(s, LB - 1))
            far = block(far_ref, jnp.maximum(s - LB, 0))
            one = jnp.where(s < LB, own, far)
            ones.append(jnp.where(d >= 0, one, jnp.zeros_like(one)))
        sums.append(mm(jnp.concatenate([mats_ref[0, t] for t in tiles], axis=1), jnp.concatenate(ones, axis=0)))
    for j in range(HBLK):
        part = mm(mats_ref[0, LOCAL + j], far_ref[j * BLK : (j + 1) * BLK, :])
        d = dst_ref[0, LOCAL + j]
        for b in range(LB):
            sums[b] = sums[b] + jnp.where(d == b, part, 0.0)
    return sums


def agg_kernel(dst_ref, src_ref, mats_ref, x_ref, halo_ref, *refs):
    out_ref = refs[-1]
    sums = tile_sums(dst_ref, src_ref, mats_ref, x_ref, halo_ref)
    for b in range(LB):
        value = sums[b].astype(bf16)
        for c in range(N_CACHE):
            out_ref[c, b * BLK : (b + 1) * BLK, :] = value


def side_kernel(
    me_ref, dst_ref, src_ref, mats_ref, s2_ref, n2_ref, b2_ref, p0, p1, p2, p3, out_hbm,
    lhs, far, rest, packs, out, sems,
):
    width = n2_ref.shape[1]
    rows = rest.shape[0]
    after = 3 * rows + 16
    depth = (p0.shape[0] - after) // N_CACHE
    refs = (p0, p1, p2, p3)
    copies = []
    for i, part in enumerate((pl.ds(after, N_CACHE * depth), pl.ds(0, after))):
        for k, ref in enumerate(refs):
            copies.append(pltpu.make_async_copy(ref.at[part, :], packs.at[k, part, :], sems.at[k, i]))
            copies[-1].start()
    peers = peers_of(me_ref[0])
    n2 = n2_ref[...]
    for k in range(N_CACHE):
        copies[k].wait()
        parts = [packs[k, after + c * depth : after + (c + 1) * depth, :] for c in range(N_CACHE)]
        value = mm(jnp.concatenate(parts, axis=1), n2).astype(bf16)
        far[pl.ds(pl.multiple_of(peers[k] * depth, 128), depth), :] = value
    sums = [jnp.broadcast_to(b2_ref[...], (BLK, width))] * LB
    for j in range(HBLK):
        part = mm(mats_ref[0, LOCAL + j], far[j * BLK : (j + 1) * BLK, :])
        d = dst_ref[0, LOCAL + j]
        for b in range(LB):
            sums[b] = sums[b] + jnp.where(d == b, part, 0.0)
    for b in range(LB):
        rest[b * BLK : (b + 1) * BLK, :] = sums[b]
    for t in range(LOCAL):
        d, s = dst_ref[0, t], src_ref[0, t]

        @pl.when((d >= 0) & (s >= LB))
        def _():
            part = slice(t // 4 * BLK, (t // 4 + 1) * BLK)
            rest[part, :] += mm(mats_ref[0, t], block(far, s - LB))

    full = N_CACHE * width
    out[:rows, 2 * full + 2 * width :] = rest[...].astype(bf16)
    marks = []
    for t in range(LOCAL):
        d, s = dst_ref[0, t], src_ref[0, t]
        for i in range(LB):
            marks.append(jnp.full((1, width), jnp.where((d >= 0) & (s == i), 1.0, 0.0), f32))
    out[rows:, 2 * full + 2 * width :] = jnp.concatenate(marks, axis=0).astype(bf16)

    for k in range(N_CACHE):
        copies[N_CACHE + k].wait()
        lhs[:, pl.ds(pl.multiple_of(peers[k] * width, width), width)] = packs[k, 2 * rows : 3 * rows, :]
        out[:rows, full + k * width : full + (k + 1) * width] = packs[k, rows : 2 * rows, :]
        for i, ref in enumerate((s2_ref, n2_ref)):
            value = ref[pl.ds(pl.multiple_of(peers[k] * width, width), width), :]
            out[k * width : (k + 1) * width, 2 * full + i * width : 2 * full + (i + 1) * width] = value
    terms = [packs[k, 3 * rows : after, :].astype(f32) for k in range(N_CACHE)]
    bias = jnp.concatenate([t[0:1] + t[1:2] + t[2:3] for t in terms], axis=1)
    ws = jnp.concatenate([packs[k, :rows, :] for k in range(N_CACHE)], axis=1)
    out[:rows, :full] = (mm(lhs[...], ws) + bias).astype(bf16)
    last = pltpu.make_async_copy(out, out_hbm, sems.at[0, 0])
    last.start()
    last.wait()


def last_kernel(used_ref, full_hbm, mats_hbm, side_hbm, out_ref, full_ref, mats, side, z, sems):
    rows, width = out_ref.shape
    whole = N_CACHE * width
    copies = []
    for i, part in enumerate((pl.ds(0, 2 * whole), pl.ds(2 * whole, 3 * width))):
        copies.append(pltpu.make_async_copy(side_hbm.at[:, part], side.at[:, part], sems.at[i]))
    copies.append(pltpu.make_async_copy(mats_hbm.at[0, pl.ds(0, LOCAL)], mats, sems.at[2]))
    copies.append(pltpu.make_async_copy(full_hbm, full_ref, sems.at[3]))
    for copy in copies[3:] + copies[:3]:
        copy.start()
    copies[3].wait()
    agg = jnp.concatenate([full_ref[c] for c in range(N_CACHE)], axis=1)
    copies[0].wait()
    wide = jnp.maximum(side[:rows, :whole].astype(f32) + mm(agg, side[:rows, whole : 2 * whole]), 0.0)
    scale = lax.rsqrt(jnp.sum(wide * wide, axis=1, keepdims=True) / whole + epsilon)
    copies[1].wait()
    both = mm(wide.astype(bf16), side[:rows, 2 * whole : 2 * whole + 2 * width]) * scale
    z[...] = both[:, width:].astype(bf16)
    copies[2].wait()
    marks = side[rows:, 2 * whole + 2 * width :]
    for b in range(LB):
        part = slice(b * BLK, (b + 1) * BLK)
        value = both[part, :width] + side[part, 2 * whole + 2 * width :].astype(f32)
        tiles = range(4 * b, 4 * b + 4)
        ones = [z[:BLK, :] * marks[2 * t : 2 * t + 1] + z[BLK:, :] * marks[2 * t + 1 : 2 * t + 2] for t in tiles]
        value = value + mm(
            jnp.concatenate([mats[t] for t in tiles], axis=1), jnp.concatenate(ones, axis=0)
        )
        out_ref[part, :] = jnp.where(b < used_ref[0], value, 0.0).astype(bf16)


def body(
    x, used, send_rows, tile_dst, tile_src, mats, history,
    self_one, neigh_one, bias_one, self_two, neigh_two, bias_two,
):
    rows, width = x.shape
    depth = history.shape[0]
    dests = send_rows.shape[1]
    me = lax.axis_index("cache").astype(jnp.int32).reshape(1)
    shape = jax.ShapeDtypeStruct
    spread = dict(split_axis=0, concat_axis=0, tiled=True)
    bias = bias_one.reshape(1, -1)

    length = 3 * rows + 16 + N_CACHE * depth
    pack = call(
        pack_kernel, shape((length, width), bf16), [ANY] * 5,
        [pltpu.VMEM((1, width), f32), pltpu.VMEM((length, width), bf16), pltpu.SemaphoreType.DMA((9,))],
        out_specs=ANY, vmem=56,
    )(self_one, neigh_one, x, history, bias)
    sent = [
        lax.ppermute(pack, "cache", [(i, (i + d) % N_CACHE) for i in range(N_CACHE)]) for d in (1, 2, 3)
    ]
    outbound = call(
        gather_kernel, shape((dests * SLOT, width), bf16), [VMEM] * 2,
        [pltpu.VMEM((dests, dests), f32), pltpu.VMEM((dests * SLOT, width), f32)],
    )(jnp.swapaxes(send_rows, 1, 2), x)
    halo = lax.cond(
        used[0] > 0,
        lambda v: lax.all_to_all(v, "dom", **spread),
        jnp.zeros_like,
        outbound.reshape(dests, SLOT // 4, 4, width),
    )
    halo = halo.reshape(dests * SLOT, width)

    full = call(
        agg_kernel, shape((N_CACHE, rows, width), bf16), [SMEM] * 2 + [VMEM] * 3, flops=10**6
    )(tile_dst, tile_src, mats, x, halo)
    full = lax.all_to_all(full, "cache", **spread)

    side = call(
        side_kernel, shape((rows + 16, (2 * N_CACHE + 3) * width), bf16),
        [SMEM] * 3 + [VMEM] * 4 + [ANY] * 4,
        [
            pltpu.VMEM((rows, N_CACHE * width), bf16),
            pltpu.VMEM((HBLK * BLK, width), bf16),
            pltpu.VMEM((rows, width), f32),
            pltpu.VMEM((N_CACHE, length, width), bf16),
            pltpu.VMEM((rows + 16, (2 * N_CACHE + 3) * width), bf16),
            pltpu.SemaphoreType.DMA((N_CACHE, 2)),
        ], out_specs=ANY, flops=10**9, vmem=58,
    )(me, tile_dst, tile_src, mats, self_two, neigh_two, bias_two.reshape(1, -1), pack, *sent)

    return call(
        last_kernel, shape((rows, width), bf16), [SMEM, ANY, ANY, ANY],
        [
            pltpu.VMEM((N_CACHE, rows, width), bf16),
            pltpu.VMEM((LOCAL, BLK, BLK), bf16),
            pltpu.VMEM((rows + 16, (2 * N_CACHE + 3) * width), bf16),
            pltpu.VMEM((rows, width), bf16),
            pltpu.SemaphoreType.DMA((4,)),
        ], vmem=53,
    )(used, full, mats, side)


def solution(mesh):
    return jax.shard_map(
        body,
        mesh=mesh,
        in_specs=(
            P("dom", "cache"),
            P("dom"),
            P("dom", None, None),
            P("dom", None),
            P("dom", None),
            P("dom", None, None, None),
            P(("dom", "cache"), None),
            P(None, "cache"),
            P(None, "cache"),
            P("cache"),
            P(None, "cache"),
            P(None, "cache"),
            P("cache"),
        ),
        out_specs=P("dom", "cache"),
        check_vma=False,
    )
```

```python
import jax
import jax.numpy as jnp
from jax import lax
from jax.experimental import pallas as pl
from jax.experimental.pallas import tpu as pltpu
from jax.sharding import PartitionSpec as P

epsilon = 1e-06
ANY = pl.BlockSpec(memory_space=pl.ANY)
VMEM = pl.BlockSpec(memory_space=pltpu.VMEM)
SMEM = pl.BlockSpec(memory_space=pltpu.SMEM)
f32, bf16 = jnp.float32, jnp.bfloat16
LB, BLK, HBLK, LOCAL, SLOT = 2, 256, 6, 8, 12
N_CACHE = 4


def call(kernel, out_shape, in_specs, scratch=(), out_specs=None, vmem=16, flops=2 * 10**10):
    return pl.pallas_call(
        kernel,
        out_shape=out_shape,
        in_specs=in_specs,
        out_specs=out_specs or jax.tree.map(lambda _: VMEM, out_shape),
        scratch_shapes=list(scratch),
        compiler_params=pltpu.CompilerParams(vmem_limit_bytes=vmem * 2**20),
        cost_estimate=pl.CostEstimate(flops=flops, bytes_accessed=10**6, transcendentals=0),
    )


def mm(a, b):
    return jnp.dot(a, b, preferred_element_type=f32)


def block(ref, i):
    return ref[pl.ds(pl.multiple_of(i * BLK, BLK), BLK), :]


def peers_of(me):
    return [me] + [lax.rem(me + N_CACHE - d, N_CACHE) for d in (1, 2, 3)]


def pack_kernel(ws_hbm, wn_hbm, x_hbm, hist_hbm, b_hbm, pack_hbm, b_ref, wide, sems):
    load = pltpu.make_async_copy(b_hbm, b_ref, sems.at[0])
    load.start()
    rows, width = x_hbm.shape
    parts = [(ref, k * rows) for k, ref in enumerate((ws_hbm, wn_hbm, x_hbm))]
    tail = 3 * rows
    for k in range(N_CACHE):
        parts.append((hist_hbm.at[:, pl.ds(k * width, width)], tail + 16 + k * hist_hbm.shape[0]))
    copies = []
    for k, (ref, at) in enumerate(parts):
        copies.append(pltpu.make_async_copy(ref, wide.at[pl.ds(at, ref.shape[0]), :], sems.at[1 + k]))
        copies[-1].start()
    load.wait()
    one, terms = b_ref[...], []
    for _ in range(3):
        terms.append(one.astype(bf16))
        one = one - terms[-1].astype(f32)
    wide[tail : tail + 16, :] = jnp.concatenate(terms + [jnp.zeros((13, width), bf16)], axis=0)
    outs = []

    def send(at, size):
        part = pl.ds(at, size)
        outs.append(pltpu.make_async_copy(wide.at[part, :], pack_hbm.at[part, :], sems.at[8 + len(outs)]))
        outs[-1].start()

    send(tail, 16)
    for copy, (ref, at) in zip(copies, parts):
        copy.wait()
        send(at, ref.shape[0])
    for copy in outs:
        copy.wait()


def gather_kernel(rows_ref, x_ref, out_ref, square, wide):
    dests = rows_ref.shape[2]
    square[...] = jnp.zeros_like(square)
    square[:SLOT, :] = rows_ref[0].astype(f32)
    rows = square[...].T.astype(jnp.int32)
    lanes = lax.broadcasted_iota(jnp.int32, (dests, x_ref.shape[0]), 1)
    x = x_ref[...]
    for s in range(SLOT):
        onehot = (lanes == rows[:, s : s + 1]).astype(f32).astype(bf16)
        wide[pl.ds(s, dests, stride=SLOT), :] = mm(onehot, x)
    out_ref[...] = wide[: dests * SLOT, :].astype(bf16)


def agg_kernel(dst_ref, src_ref, mats_ref, x_ref, halo_ref, out_hbm, parts, out, sems):
    for j in range(HBLK):
        parts[j * BLK : (j + 1) * BLK, :] = mm(mats_ref[0, LOCAL + j], halo_ref[j * BLK : (j + 1) * BLK, :])
    copies = []
    for b in range(LB):
        tiles, ones = range(4 * b, 4 * b + 4), []
        for t in tiles:
            d, s = dst_ref[0, t], src_ref[0, t]
            own = block(x_ref, jnp.minimum(s, LB - 1))
            far = block(halo_ref, jnp.maximum(s - LB, 0))
            one = jnp.where(s < LB, own, far)
            ones.append(jnp.where(d >= 0, one, jnp.zeros_like(one)))
        total = mm(jnp.concatenate([mats_ref[0, t] for t in tiles], axis=1), jnp.concatenate(ones, axis=0))
        for j in range(HBLK):
            total = total + jnp.where(dst_ref[0, LOCAL + j] == b, parts[j * BLK : (j + 1) * BLK, :], 0.0)
        rows = pl.ds(b * BLK, BLK)
        out[b * BLK : (b + 1) * BLK, :] = total.astype(bf16)
        for c in range(N_CACHE):
            copies.append(pltpu.make_async_copy(out.at[rows, :], out_hbm.at[c, rows, :], sems.at[b, c]))
            copies[-1].start()
    for copy in copies:
        copy.wait()


def side_kernel(
    me_ref, dst_ref, src_ref, mats_ref, s2_ref, n2_ref, b2_ref, p0, p1, p2, p3, out_hbm,
    lhs, far, rest, packs, out, sems,
):
    width = n2_ref.shape[1]
    rows = rest.shape[0]
    after = 3 * rows + 16
    depth = (p0.shape[0] - after) // N_CACHE
    refs = (p0, p1, p2, p3)
    copies = []
    for i, part in enumerate((pl.ds(after, N_CACHE * depth), pl.ds(0, after))):
        for k, ref in enumerate(refs):
            copies.append(pltpu.make_async_copy(ref.at[part, :], packs.at[k, part, :], sems.at[k, i]))
            copies[-1].start()
    peers = peers_of(me_ref[0])
    n2 = n2_ref[...]
    for k in range(N_CACHE):
        copies[k].wait()
        parts = [packs[k, after + c * depth : after + (c + 1) * depth, :] for c in range(N_CACHE)]
        value = mm(jnp.concatenate(parts, axis=1), n2).astype(bf16)
        far[pl.ds(pl.multiple_of(peers[k] * depth, 128), depth), :] = value
    sums = [jnp.broadcast_to(b2_ref[...], (BLK, width))] * LB
    for j in range(HBLK):
        part = mm(mats_ref[0, LOCAL + j], far[j * BLK : (j + 1) * BLK, :])
        d = dst_ref[0, LOCAL + j]
        for b in range(LB):
            sums[b] = sums[b] + jnp.where(d == b, part, 0.0)
    for b in range(LB):
        rest[b * BLK : (b + 1) * BLK, :] = sums[b]
    for t in range(LOCAL):
        d, s = dst_ref[0, t], src_ref[0, t]

        @pl.when((d >= 0) & (s >= LB))
        def _():
            part = slice(t // 4 * BLK, (t // 4 + 1) * BLK)
            rest[part, :] += mm(mats_ref[0, t], block(far, s - LB))

    full = N_CACHE * width
    out[:rows, 2 * full + 2 * width :] = rest[...].astype(bf16)
    marks = []
    for t in range(LOCAL):
        d, s = dst_ref[0, t], src_ref[0, t]
        for i in range(LB):
            marks.append(jnp.full((1, width), jnp.where((d >= 0) & (s == i), 1.0, 0.0), f32))
    out[rows:, 2 * full + 2 * width :] = jnp.concatenate(marks, axis=0).astype(bf16)

    for k in range(N_CACHE):
        copies[N_CACHE + k].wait()
        lhs[:, pl.ds(pl.multiple_of(peers[k] * width, width), width)] = packs[k, 2 * rows : 3 * rows, :]
        out[:rows, full + k * width : full + (k + 1) * width] = packs[k, rows : 2 * rows, :]
        for i, ref in enumerate((s2_ref, n2_ref)):
            value = ref[pl.ds(pl.multiple_of(peers[k] * width, width), width), :]
            out[k * width : (k + 1) * width, 2 * full + i * width : 2 * full + (i + 1) * width] = value
    terms = [packs[k, 3 * rows : after, :].astype(f32) for k in range(N_CACHE)]
    bias = jnp.concatenate([t[0:1] + t[1:2] + t[2:3] for t in terms], axis=1)
    ws = jnp.concatenate([packs[k, :rows, :] for k in range(N_CACHE)], axis=1)
    out[:rows, :full] = (mm(lhs[...], ws) + bias).astype(bf16)
    last = pltpu.make_async_copy(out, out_hbm, sems.at[0, 0])
    last.start()
    last.wait()


def last_kernel(used_ref, full_ref, mats_hbm, side_hbm, out_ref, mats, side, base, z, sems):
    rows, width = out_ref.shape
    whole = N_CACHE * width
    copies = []
    for i, part in enumerate((pl.ds(whole, whole), pl.ds(0, whole), pl.ds(2 * whole, 3 * width))):
        copies.append(pltpu.make_async_copy(side_hbm.at[:, part], side.at[:, part], sems.at[i]))
    copies.append(pltpu.make_async_copy(mats_hbm.at[0, pl.ds(0, LOCAL)], mats, sems.at[3]))
    for copy in copies:
        copy.start()
    for copy in copies[:3]:
        copy.wait()
    second = side[:rows, 2 * whole : 2 * whole + 2 * width]
    for b in range(LB):
        part = slice(b * BLK, (b + 1) * BLK)
        agg = jnp.concatenate([full_ref[c, part, :] for c in range(N_CACHE)], axis=1)
        wide = jnp.maximum(side[part, :whole].astype(f32) + mm(agg, side[:rows, whole : 2 * whole]), 0.0)
        scale = lax.rsqrt(jnp.sum(wide * wide, axis=1, keepdims=True) / whole + epsilon)
        both = mm(wide.astype(bf16), second) * scale
        base[part, :] = both[:, :width] + side[part, 2 * whole + 2 * width :].astype(f32)
        z[part, :] = both[:, width:].astype(bf16)
    copies[3].wait()
    marks = side[rows:, 2 * whole + 2 * width :]
    for b in range(LB):
        part = slice(b * BLK, (b + 1) * BLK)
        tiles = range(4 * b, 4 * b + 4)
        ones = [z[:BLK, :] * marks[2 * t : 2 * t + 1] + z[BLK:, :] * marks[2 * t + 1 : 2 * t + 2] for t in tiles]
        value = base[part, :] + mm(
            jnp.concatenate([mats[t] for t in tiles], axis=1), jnp.concatenate(ones, axis=0)
        )
        out_ref[part, :] = jnp.where(b < used_ref[0], value, 0.0).astype(bf16)


def body(
    x, used, send_rows, tile_dst, tile_src, mats, history,
    self_one, neigh_one, bias_one, self_two, neigh_two, bias_two,
):
    rows, width = x.shape
    depth = history.shape[0]
    dests = send_rows.shape[1]
    me = lax.axis_index("cache").astype(jnp.int32).reshape(1)
    shape = jax.ShapeDtypeStruct
    spread = dict(split_axis=0, concat_axis=0, tiled=True)
    bias = bias_one.reshape(1, -1)

    length = 3 * rows + 16 + N_CACHE * depth
    pack = call(
        pack_kernel, shape((length, width), bf16), [ANY] * 5,
        [pltpu.VMEM((1, width), f32), pltpu.VMEM((length, width), bf16), pltpu.SemaphoreType.DMA((16,))],
        out_specs=ANY, vmem=56,
    )(self_one, neigh_one, x, history, bias)
    sent = [
        lax.ppermute(pack, "cache", [(i, (i + d) % N_CACHE) for i in range(N_CACHE)]) for d in (1, 2, 3)
    ]
    outbound = call(
        gather_kernel, shape((dests * SLOT, width), bf16), [VMEM] * 2,
        [pltpu.VMEM((dests, dests), f32), pltpu.VMEM((dests * SLOT + 16, width), f32)],
    )(jnp.swapaxes(send_rows, 1, 2), x)
    halo = lax.cond(
        me[0] < N_CACHE,
        lambda v: lax.all_to_all(v, "dom", **spread),
        jnp.zeros_like,
        outbound.reshape(dests, SLOT // 4, 4, width),
    )
    halo = halo.reshape(dests * SLOT, width)

    full = call(
        agg_kernel, shape((N_CACHE, rows, width), bf16), [SMEM] * 2 + [VMEM] * 3,
        [
            pltpu.VMEM((HBLK * BLK, width), f32),
            pltpu.VMEM((rows, width), bf16),
            pltpu.SemaphoreType.DMA((LB, N_CACHE)),
        ], out_specs=ANY, flops=10**6
    )(tile_dst, tile_src, mats, x, halo)
    full = lax.all_to_all(full, "cache", **spread)

    side = call(
        side_kernel, shape((rows + 16, (2 * N_CACHE + 3) * width), bf16),
        [SMEM] * 3 + [VMEM] * 4 + [ANY] * 4,
        [
            pltpu.VMEM((rows, N_CACHE * width), bf16),
            pltpu.VMEM((HBLK * BLK, width), bf16),
            pltpu.VMEM((rows, width), f32),
            pltpu.VMEM((N_CACHE, length, width), bf16),
            pltpu.VMEM((rows + 16, (2 * N_CACHE + 3) * width), bf16),
            pltpu.SemaphoreType.DMA((N_CACHE, 2)),
        ], out_specs=ANY, flops=10**9, vmem=58,
    )(me, tile_dst, tile_src, mats, self_two, neigh_two, bias_two.reshape(1, -1), pack, *sent)

    return call(
        last_kernel, shape((rows, width), bf16), [SMEM, VMEM, ANY, ANY],
        [
            pltpu.VMEM((LOCAL, BLK, BLK), bf16),
            pltpu.VMEM((rows + 16, (2 * N_CACHE + 3) * width), bf16),
            pltpu.VMEM((rows, width), f32),
            pltpu.VMEM((rows, width), bf16),
            pltpu.SemaphoreType.DMA((4,)),
        ], vmem=53,
    )(used, full, mats, side)


def solution(mesh):
    return jax.shard_map(
        body,
        mesh=mesh,
        in_specs=(
            P("dom", "cache"),
            P("dom"),
            P("dom", None, None),
            P("dom", None),
            P("dom", None),
            P("dom", None, None, None),
            P(("dom", "cache"), None),
            P(None, "cache"),
            P(None, "cache"),
            P("cache"),
            P(None, "cache"),
            P(None, "cache"),
            P("cache"),
        ),
        out_specs=P("dom", "cache"),
        check_vma=False,
    )
```

```python
import jax
import jax.numpy as jnp
from jax import lax
from jax.experimental import pallas as pl
from jax.experimental.pallas import tpu as pltpu
from jax.sharding import PartitionSpec as P

epsilon = 1e-06
ANY = pl.BlockSpec(memory_space=pl.ANY)
VMEM = pl.BlockSpec(memory_space=pltpu.VMEM)
SMEM = pl.BlockSpec(memory_space=pltpu.SMEM)
f32, bf16 = jnp.float32, jnp.bfloat16
LB, BLK, HBLK, LOCAL, SLOT = 2, 256, 6, 8, 12
N_CACHE = 4


def call(kernel, out_shape, in_specs, scratch=(), out_specs=None, vmem=16, flops=2 * 10**10):
    return pl.pallas_call(
        kernel,
        out_shape=out_shape,
        in_specs=in_specs,
        out_specs=out_specs or jax.tree.map(lambda _: VMEM, out_shape),
        scratch_shapes=list(scratch),
        compiler_params=pltpu.CompilerParams(vmem_limit_bytes=vmem * 2**20),
        cost_estimate=pl.CostEstimate(flops=flops, bytes_accessed=10**6, transcendentals=0),
    )


def mm(a, b):
    return jnp.dot(a, b, preferred_element_type=f32)


def block(ref, i):
    return ref[pl.ds(pl.multiple_of(i * BLK, BLK), BLK), :]


def peers_of(me):
    return [me] + [lax.rem(me + N_CACHE - d, N_CACHE) for d in (1, 2, 3)]


def first_kernel(
    ws_hbm, wn_hbm, x_hbm, hist_hbm, b_hbm, rows_hbm, pack_hbm, bound_hbm,
    b_ref, rows_ref, wide, square, picked, bound, sems,
):
    load = pltpu.make_async_copy(b_hbm, b_ref, sems.at[0])
    load.start()
    load_rows = pltpu.make_async_copy(rows_hbm, rows_ref, sems.at[16])
    load_rows.start()
    rows, width = x_hbm.shape
    parts = [(x_hbm, 2 * rows), (ws_hbm, 0), (wn_hbm, rows)]
    tail = 3 * rows
    for k in range(N_CACHE):
        parts.append((hist_hbm.at[:, pl.ds(k * width, width)], tail + 16 + k * hist_hbm.shape[0]))
    copies = []
    for k, (ref, at) in enumerate(parts):
        copies.append(pltpu.make_async_copy(ref, wide.at[pl.ds(at, ref.shape[0]), :], sems.at[1 + k]))
        copies[-1].start()
    load.wait()
    one, terms = b_ref[...], []
    for _ in range(3):
        terms.append(one.astype(bf16))
        one = one - terms[-1].astype(f32)
    wide[tail : tail + 16, :] = jnp.concatenate(terms + [jnp.zeros((13, width), bf16)], axis=0)
    outs = []

    def send(at, size):
        part = pl.ds(at, size)
        outs.append(pltpu.make_async_copy(wide.at[part, :], pack_hbm.at[part, :], sems.at[8 + len(outs)]))
        outs[-1].start()

    send(tail, 16)
    for copy, (ref, at) in zip(copies, parts):
        copy.wait()
        send(at, ref.shape[0])
    load_rows.wait()
    dests = rows_ref.shape[2]
    square[...] = jnp.zeros_like(square)
    square[:SLOT, :] = rows_ref[:, 0, :].astype(f32)
    wanted = square[...].T.astype(jnp.int32)
    lanes = lax.broadcasted_iota(jnp.int32, (dests, rows), 1)
    x = wide[2 * rows : 3 * rows, :]
    for s in range(SLOT):
        onehot = (lanes == wanted[:, s : s + 1]).astype(f32).astype(bf16)
        picked[pl.ds(s, dests, stride=SLOT), :] = mm(onehot, x)
    bound[...] = picked[: dests * SLOT, :].astype(bf16)
    outs.append(pltpu.make_async_copy(bound, bound_hbm, sems.at[17]))
    outs[-1].start()
    for copy in outs:
        copy.wait()


def agg_kernel(dst_ref, src_ref, mats_ref, x_ref, halo_ref, out_hbm, parts, out, sems):
    for j in range(HBLK):
        parts[j * BLK : (j + 1) * BLK, :] = mm(mats_ref[0, LOCAL + j], halo_ref[j * BLK : (j + 1) * BLK, :])
    copies = []
    for b in range(LB):
        tiles, ones = range(4 * b, 4 * b + 4), []
        for t in tiles:
            d, s = dst_ref[0, t], src_ref[0, t]
            own = block(x_ref, jnp.minimum(s, LB - 1))
            far = block(halo_ref, jnp.maximum(s - LB, 0))
            one = jnp.where(s < LB, own, far)
            ones.append(jnp.where(d >= 0, one, jnp.zeros_like(one)))
        total = mm(jnp.concatenate([mats_ref[0, t] for t in tiles], axis=1), jnp.concatenate(ones, axis=0))
        for j in range(HBLK):
            total = total + jnp.where(dst_ref[0, LOCAL + j] == b, parts[j * BLK : (j + 1) * BLK, :], 0.0)
        rows = pl.ds(b * BLK, BLK)
        out[b * BLK : (b + 1) * BLK, :] = total.astype(bf16)
        for c in range(N_CACHE):
            copies.append(pltpu.make_async_copy(out.at[rows, :], out_hbm.at[c, rows, :], sems.at[b, c]))
            copies[-1].start()
    for copy in copies:
        copy.wait()


def side_kernel(
    me_ref, dst_ref, src_ref, mats_ref, s2_ref, n2_ref, b2_ref, p0, p1, p2, p3, out_hbm,
    lhs, far, rest, packs, out, sems,
):
    width = n2_ref.shape[1]
    rows = rest.shape[0]
    after = 3 * rows + 16
    depth = (p0.shape[0] - after) // N_CACHE
    refs = (p0, p1, p2, p3)
    copies = []
    for i, part in enumerate((pl.ds(after, N_CACHE * depth), pl.ds(0, after))):
        for k, ref in enumerate(refs):
            copies.append(pltpu.make_async_copy(ref.at[part, :], packs.at[k, part, :], sems.at[k, i]))
            copies[-1].start()
    peers = peers_of(me_ref[0])
    n2 = n2_ref[...]
    for k in range(N_CACHE):
        copies[k].wait()
        parts = [packs[k, after + c * depth : after + (c + 1) * depth, :] for c in range(N_CACHE)]
        value = mm(jnp.concatenate(parts, axis=1), n2).astype(bf16)
        far[pl.ds(pl.multiple_of(peers[k] * depth, 128), depth), :] = value
    sums = [jnp.broadcast_to(b2_ref[...], (BLK, width))] * LB
    for j in range(HBLK):
        part = mm(mats_ref[0, LOCAL + j], far[j * BLK : (j + 1) * BLK, :])
        d = dst_ref[0, LOCAL + j]
        for b in range(LB):
            sums[b] = sums[b] + jnp.where(d == b, part, 0.0)
    for b in range(LB):
        rest[b * BLK : (b + 1) * BLK, :] = sums[b]
    for t in range(LOCAL):
        d, s = dst_ref[0, t], src_ref[0, t]

        @pl.when((d >= 0) & (s >= LB))
        def _():
            part = slice(t // 4 * BLK, (t // 4 + 1) * BLK)
            rest[part, :] += mm(mats_ref[0, t], block(far, s - LB))

    full = N_CACHE * width
    out[:rows, 2 * full + 2 * width :] = rest[...].astype(bf16)
    marks = []
    for t in range(LOCAL):
        d, s = dst_ref[0, t], src_ref[0, t]
        for i in range(LB):
            marks.append(jnp.full((1, width), jnp.where((d >= 0) & (s == i), 1.0, 0.0), f32))
    out[rows:, 2 * full + 2 * width :] = jnp.concatenate(marks, axis=0).astype(bf16)

    for k in range(N_CACHE):
        copies[N_CACHE + k].wait()
        lhs[:, pl.ds(pl.multiple_of(peers[k] * width, width), width)] = packs[k, 2 * rows : 3 * rows, :]
        out[:rows, full + k * width : full + (k + 1) * width] = packs[k, rows : 2 * rows, :]
        for i, ref in enumerate((s2_ref, n2_ref)):
            value = ref[pl.ds(pl.multiple_of(peers[k] * width, width), width), :]
            out[k * width : (k + 1) * width, 2 * full + i * width : 2 * full + (i + 1) * width] = value
    terms = [packs[k, 3 * rows : after, :].astype(f32) for k in range(N_CACHE)]
    bias = jnp.concatenate([t[0:1] + t[1:2] + t[2:3] for t in terms], axis=1)
    ws = jnp.concatenate([packs[k, :rows, :] for k in range(N_CACHE)], axis=1)
    out[:rows, :full] = (mm(lhs[...], ws) + bias).astype(bf16)
    last = pltpu.make_async_copy(out, out_hbm, sems.at[0, 0])
    last.start()
    last.wait()


def last_kernel(used_ref, full_ref, mats_hbm, side_hbm, out_ref, mats, side, base, z, sems):
    rows, width = out_ref.shape
    whole = N_CACHE * width
    copies = []
    for i, part in enumerate((pl.ds(whole, whole), pl.ds(0, whole), pl.ds(2 * whole, 3 * width))):
        copies.append(pltpu.make_async_copy(side_hbm.at[:, part], side.at[:, part], sems.at[i]))
    copies.append(pltpu.make_async_copy(mats_hbm.at[0, pl.ds(0, LOCAL)], mats, sems.at[3]))
    for copy in copies:
        copy.start()
    copies[0].wait()
    for b in range(LB):
        part = slice(b * BLK, (b + 1) * BLK)
        agg = jnp.concatenate([full_ref[c, part, :] for c in range(N_CACHE)], axis=1)
        wide = mm(agg, side[:rows, whole : 2 * whole])
        if b == 0:
            copies[1].wait()
        wide = jnp.maximum(side[part, :whole].astype(f32) + wide, 0.0)
        scale = lax.rsqrt(jnp.sum(wide * wide, axis=1, keepdims=True) / whole + epsilon)
        if b == 0:
            copies[2].wait()
        both = mm(wide.astype(bf16), side[:rows, 2 * whole : 2 * whole + 2 * width]) * scale
        base[part, :] = both[:, :width] + side[part, 2 * whole + 2 * width :].astype(f32)
        z[part, :] = both[:, width:].astype(bf16)
    copies[3].wait()
    marks = side[rows:, 2 * whole + 2 * width :]
    for b in range(LB):
        part = slice(b * BLK, (b + 1) * BLK)
        tiles = range(4 * b, 4 * b + 4)
        ones = [z[:BLK, :] * marks[2 * t : 2 * t + 1] + z[BLK:, :] * marks[2 * t + 1 : 2 * t + 2] for t in tiles]
        value = base[part, :] + mm(
            jnp.concatenate([mats[t] for t in tiles], axis=1), jnp.concatenate(ones, axis=0)
        )
        out_ref[part, :] = jnp.where(b < used_ref[0], value, 0.0).astype(bf16)


def body(
    x, used, send_rows, tile_dst, tile_src, mats, history,
    self_one, neigh_one, bias_one, self_two, neigh_two, bias_two,
):
    rows, width = x.shape
    depth = history.shape[0]
    dests = send_rows.shape[1]
    me = lax.axis_index("cache").astype(jnp.int32).reshape(1)
    shape = jax.ShapeDtypeStruct
    spread = dict(split_axis=0, concat_axis=0, tiled=True)
    bias = bias_one.reshape(1, -1)

    length = 3 * rows + 16 + N_CACHE * depth
    pack, outbound = call(
        first_kernel,
        [shape((length, width), bf16), shape((dests * SLOT, width), bf16)], [ANY] * 6,
        [
            pltpu.VMEM((1, width), f32),
            pltpu.VMEM((SLOT, 1, dests), jnp.int32),
            pltpu.VMEM((length, width), bf16),
            pltpu.VMEM((dests, dests), f32),
            pltpu.VMEM((dests * SLOT + 16, width), f32),
            pltpu.VMEM((dests * SLOT, width), bf16),
            pltpu.SemaphoreType.DMA((18,)),
        ],
        out_specs=[ANY] * 2, vmem=56,
    )(self_one, neigh_one, x, history, bias, jnp.transpose(send_rows, (2, 0, 1)))
    sent = [
        lax.ppermute(pack, "cache", [(i, (i + d) % N_CACHE) for i in range(N_CACHE)]) for d in (1, 2, 3)
    ]
    halo = lax.cond(
        me[0] < N_CACHE,
        lambda v: lax.all_to_all(v, "dom", **spread),
        jnp.zeros_like,
        outbound.reshape(dests, SLOT // 4, 4, width),
    )
    halo = halo.reshape(dests * SLOT, width)

    full = call(
        agg_kernel, shape((N_CACHE, rows, width), bf16), [SMEM] * 2 + [VMEM] * 3,
        [
            pltpu.VMEM((HBLK * BLK, width), f32),
            pltpu.VMEM((rows, width), bf16),
            pltpu.SemaphoreType.DMA((LB, N_CACHE)),
        ], out_specs=ANY, flops=10**6
    )(tile_dst, tile_src, mats, x, halo)
    full = lax.all_to_all(full, "cache", **spread)

    side = call(
        side_kernel, shape((rows + 16, (2 * N_CACHE + 3) * width), bf16),
        [SMEM] * 3 + [VMEM] * 4 + [ANY] * 4,
        [
            pltpu.VMEM((rows, N_CACHE * width), bf16),
            pltpu.VMEM((HBLK * BLK, width), bf16),
            pltpu.VMEM((rows, width), f32),
            pltpu.VMEM((N_CACHE, length, width), bf16),
            pltpu.VMEM((rows + 16, (2 * N_CACHE + 3) * width), bf16),
            pltpu.SemaphoreType.DMA((N_CACHE, 2)),
        ], out_specs=ANY, flops=10**9, vmem=58,
    )(me, tile_dst, tile_src, mats, self_two, neigh_two, bias_two.reshape(1, -1), pack, *sent)

    return call(
        last_kernel, shape((rows, width), bf16), [SMEM, VMEM, ANY, ANY],
        [
            pltpu.VMEM((LOCAL, BLK, BLK), bf16),
            pltpu.VMEM((rows + 16, (2 * N_CACHE + 3) * width), bf16),
            pltpu.VMEM((rows, width), f32),
            pltpu.VMEM((rows, width), bf16),
            pltpu.SemaphoreType.DMA((4,)),
        ], vmem=53,
    )(used, full, mats, side)


def solution(mesh):
    return jax.shard_map(
        body,
        mesh=mesh,
        in_specs=(
            P("dom", "cache"),
            P("dom"),
            P("dom", None, None),
            P("dom", None),
            P("dom", None),
            P("dom", None, None, None),
            P(("dom", "cache"), None),
            P(None, "cache"),
            P(None, "cache"),
            P("cache"),
            P(None, "cache"),
            P(None, "cache"),
            P("cache"),
        ),
        out_specs=P("dom", "cache"),
        check_vma=False,
    )
```

```python
import jax
import jax.numpy as jnp
from jax import lax
from jax.experimental import pallas as pl
from jax.experimental.pallas import tpu as pltpu
from jax.sharding import PartitionSpec as P

epsilon = 1e-06
ANY = pl.BlockSpec(memory_space=pl.ANY)
VMEM = pl.BlockSpec(memory_space=pltpu.VMEM)
SMEM = pl.BlockSpec(memory_space=pltpu.SMEM)
f32, bf16 = jnp.float32, jnp.bfloat16
LB, BLK, HBLK, LOCAL, SLOT = 2, 256, 6, 8, 12
N_CACHE = 4


def call(kernel, out_shape, in_specs, scratch=(), out_specs=None, vmem=16, flops=2 * 10**10):
    return pl.pallas_call(
        kernel,
        out_shape=out_shape,
        in_specs=in_specs,
        out_specs=out_specs or jax.tree.map(lambda _: VMEM, out_shape),
        scratch_shapes=list(scratch),
        compiler_params=pltpu.CompilerParams(vmem_limit_bytes=vmem * 2**20),
        cost_estimate=pl.CostEstimate(flops=flops, bytes_accessed=10**6, transcendentals=0),
    )


def mm(a, b):
    return jnp.dot(a, b, preferred_element_type=f32)


def block(ref, i):
    return ref[pl.ds(pl.multiple_of(i * BLK, BLK), BLK), :]


def peers_of(me):
    return [me] + [lax.rem(me + N_CACHE - d, N_CACHE) for d in (1, 2, 3)]


def first_kernel(
    ws_hbm, wn_hbm, x_hbm, hist_hbm, b_hbm, rows_hbm, pack_hbm, bound_hbm,
    b_ref, rows_ref, wide, square, picked, bound, sems,
):
    load = pltpu.make_async_copy(b_hbm, b_ref, sems.at[0])
    load.start()
    load_rows = pltpu.make_async_copy(rows_hbm, rows_ref, sems.at[16])
    load_rows.start()
    rows, width = x_hbm.shape
    parts = [(x_hbm, 2 * rows), (ws_hbm, 0), (wn_hbm, rows)]
    tail = 3 * rows
    for k in range(N_CACHE):
        parts.append((hist_hbm.at[:, pl.ds(k * width, width)], tail + 16 + k * hist_hbm.shape[0]))
    copies = []
    for k, (ref, at) in enumerate(parts):
        copies.append(pltpu.make_async_copy(ref, wide.at[pl.ds(at, ref.shape[0]), :], sems.at[1 + k]))
        copies[-1].start()
    load.wait()
    one, terms = b_ref[...], []
    for _ in range(3):
        terms.append(one.astype(bf16))
        one = one - terms[-1].astype(f32)
    wide[tail : tail + 16, :] = jnp.concatenate(terms + [jnp.zeros((13, width), bf16)], axis=0)
    outs = []

    def send(at, size):
        part = pl.ds(at, size)
        outs.append(pltpu.make_async_copy(wide.at[part, :], pack_hbm.at[part, :], sems.at[8 + len(outs)]))
        outs[-1].start()

    send(tail, 16)
    for copy, (ref, at) in zip(copies, parts):
        copy.wait()
        send(at, ref.shape[0])
    load_rows.wait()
    dests = rows_ref.shape[2]
    square[...] = jnp.zeros_like(square)
    square[:SLOT, :] = rows_ref[:, 0, :].astype(f32)
    wanted = square[...].T.astype(jnp.int32)
    lanes = lax.broadcasted_iota(jnp.int32, (dests, rows), 1)
    x = wide[2 * rows : 3 * rows, :]
    for s in range(SLOT):
        onehot = (lanes == wanted[:, s : s + 1]).astype(f32).astype(bf16)
        picked[pl.ds(s, dests, stride=SLOT), :] = mm(onehot, x)
    bound[...] = picked[: dests * SLOT, :].astype(bf16)
    outs.append(pltpu.make_async_copy(bound, bound_hbm, sems.at[17]))
    outs[-1].start()
    for copy in outs:
        copy.wait()


def agg_kernel(dst_ref, src_ref, mats_ref, x_ref, halo_ref, out_hbm, parts, out, sems):
    for j in range(HBLK):
        parts[j * BLK : (j + 1) * BLK, :] = mm(mats_ref[0, LOCAL + j], halo_ref[j * BLK : (j + 1) * BLK, :])
    copies = []
    for b in range(LB):
        tiles, ones = range(4 * b, 4 * b + 4), []
        for t in tiles:
            d, s = dst_ref[0, t], src_ref[0, t]
            own = block(x_ref, jnp.minimum(s, LB - 1))
            far = block(halo_ref, jnp.maximum(s - LB, 0))
            one = jnp.where(s < LB, own, far)
            ones.append(jnp.where(d >= 0, one, jnp.zeros_like(one)))
        total = mm(jnp.concatenate([mats_ref[0, t] for t in tiles], axis=1), jnp.concatenate(ones, axis=0))
        for j in range(HBLK):
            total = total + jnp.where(dst_ref[0, LOCAL + j] == b, parts[j * BLK : (j + 1) * BLK, :], 0.0)
        rows = pl.ds(b * BLK, BLK)
        out[b * BLK : (b + 1) * BLK, :] = total.astype(bf16)
        for c in range(N_CACHE):
            copies.append(pltpu.make_async_copy(out.at[rows, :], out_hbm.at[c, rows, :], sems.at[b, c]))
            copies[-1].start()
    for copy in copies:
        copy.wait()


def side_kernel(
    me_ref, dst_ref, src_ref, mats_ref, s2_ref, n2_ref, b2_ref, p0, p1, p2, p3, out_hbm,
    lhs, far, rest, packs, out, sems,
):
    width = n2_ref.shape[1]
    rows = rest.shape[0]
    after = 3 * rows + 16
    depth = (p0.shape[0] - after) // N_CACHE
    refs = (p0, p1, p2, p3)
    copies = []
    for i, part in enumerate((pl.ds(after, N_CACHE * depth), pl.ds(0, after))):
        for k, ref in enumerate(refs):
            copies.append(pltpu.make_async_copy(ref.at[part, :], packs.at[k, part, :], sems.at[k, i]))
            copies[-1].start()
    peers = peers_of(me_ref[0])
    n2 = n2_ref[...]
    for k in range(N_CACHE):
        copies[k].wait()
        parts = [packs[k, after + c * depth : after + (c + 1) * depth, :] for c in range(N_CACHE)]
        value = mm(jnp.concatenate(parts, axis=1), n2).astype(bf16)
        far[pl.ds(pl.multiple_of(peers[k] * depth, 128), depth), :] = value
    sums = [jnp.broadcast_to(b2_ref[...], (BLK, width))] * LB
    for j in range(HBLK):
        part = mm(mats_ref[0, LOCAL + j], far[j * BLK : (j + 1) * BLK, :])
        d = dst_ref[0, LOCAL + j]
        for b in range(LB):
            sums[b] = sums[b] + jnp.where(d == b, part, 0.0)
    for b in range(LB):
        rest[b * BLK : (b + 1) * BLK, :] = sums[b]
    for t in range(LOCAL):
        d, s = dst_ref[0, t], src_ref[0, t]

        @pl.when((d >= 0) & (s >= LB))
        def _():
            part = slice(t // 4 * BLK, (t // 4 + 1) * BLK)
            rest[part, :] += mm(mats_ref[0, t], block(far, s - LB))

    out[2 * N_CACHE + 2, :rows, :] = rest[...].astype(bf16)
    marks = []
    for t in range(LOCAL):
        d, s = dst_ref[0, t], src_ref[0, t]
        for i in range(LB):
            marks.append(jnp.full((1, width), jnp.where((d >= 0) & (s == i), 1.0, 0.0), f32))
    out[2 * N_CACHE + 2, rows:, :] = jnp.concatenate(marks, axis=0).astype(bf16)

    for k in range(N_CACHE):
        copies[N_CACHE + k].wait()
        lhs[:, pl.ds(pl.multiple_of(peers[k] * width, width), width)] = packs[k, 2 * rows : 3 * rows, :]
        out[N_CACHE + k, :rows, :] = packs[k, rows : 2 * rows, :]
        for i, ref in enumerate((s2_ref, n2_ref)):
            value = ref[pl.ds(pl.multiple_of(peers[k] * width, width), width), :]
            out[2 * N_CACHE + i, k * width : (k + 1) * width, :] = value
    terms = [packs[k, 3 * rows : after, :].astype(f32) for k in range(N_CACHE)]
    bias = jnp.concatenate([t[0:1] + t[1:2] + t[2:3] for t in terms], axis=1)
    ws = jnp.concatenate([packs[k, :rows, :] for k in range(N_CACHE)], axis=1)
    first = (mm(lhs[...], ws) + bias).astype(bf16)
    for k in range(N_CACHE):
        out[k, :rows, :] = first[:, k * width : (k + 1) * width]
    last = pltpu.make_async_copy(out, out_hbm, sems.at[0, 0])
    last.start()
    last.wait()


def last_kernel(used_ref, full_ref, mats_hbm, side_hbm, out_ref, mats, side, base, z, sems):
    rows, width = out_ref.shape
    whole = N_CACHE * width
    copies = []
    for i, part in enumerate((pl.ds(N_CACHE, N_CACHE), pl.ds(0, N_CACHE), pl.ds(2 * N_CACHE, 3))):
        copies.append(pltpu.make_async_copy(side_hbm.at[part], side.at[part], sems.at[i]))
    copies.append(pltpu.make_async_copy(mats_hbm.at[0, pl.ds(0, LOCAL)], mats, sems.at[3]))
    for copy in copies:
        copy.start()
    copies[0].wait()
    for b in range(LB):
        part = slice(b * BLK, (b + 1) * BLK)
        agg = jnp.concatenate([full_ref[c, part, :] for c in range(N_CACHE)], axis=1)
        wide = mm(agg, jnp.concatenate([side[N_CACHE + c, :rows, :] for c in range(N_CACHE)], axis=1))
        if b == 0:
            copies[1].wait()
        own = jnp.concatenate([side[c, part, :] for c in range(N_CACHE)], axis=1)
        wide = jnp.maximum(own.astype(f32) + wide, 0.0)
        scale = lax.rsqrt(jnp.sum(wide * wide, axis=1, keepdims=True) / whole + epsilon)
        if b == 0:
            copies[2].wait()
        second = jnp.concatenate([side[2 * N_CACHE + i, :rows, :] for i in range(2)], axis=1)
        both = mm(wide.astype(bf16), second) * scale
        base[part, :] = both[:, :width] + side[2 * N_CACHE + 2, part, :].astype(f32)
        z[part, :] = both[:, width:].astype(bf16)
    copies[3].wait()
    marks = side[2 * N_CACHE + 2, rows:, :]
    for b in range(LB):
        part = slice(b * BLK, (b + 1) * BLK)
        tiles = range(4 * b, 4 * b + 4)
        ones = [z[:BLK, :] * marks[2 * t : 2 * t + 1] + z[BLK:, :] * marks[2 * t + 1 : 2 * t + 2] for t in tiles]
        value = base[part, :] + mm(
            jnp.concatenate([mats[t] for t in tiles], axis=1), jnp.concatenate(ones, axis=0)
        )
        out_ref[part, :] = jnp.where(b < used_ref[0], value, 0.0).astype(bf16)


def body(
    x, used, send_rows, tile_dst, tile_src, mats, history,
    self_one, neigh_one, bias_one, self_two, neigh_two, bias_two,
):
    rows, width = x.shape
    depth = history.shape[0]
    dests = send_rows.shape[1]
    me = lax.axis_index("cache").astype(jnp.int32).reshape(1)
    shape = jax.ShapeDtypeStruct
    spread = dict(split_axis=0, concat_axis=0, tiled=True)
    bias = bias_one.reshape(1, -1)

    length = 3 * rows + 16 + N_CACHE * depth
    pack, outbound = call(
        first_kernel,
        [shape((length, width), bf16), shape((dests * SLOT, width), bf16)], [ANY] * 6,
        [
            pltpu.VMEM((1, width), f32),
            pltpu.VMEM((SLOT, 1, dests), jnp.int32),
            pltpu.VMEM((length, width), bf16),
            pltpu.VMEM((dests, dests), f32),
            pltpu.VMEM((dests * SLOT + 16, width), f32),
            pltpu.VMEM((dests * SLOT, width), bf16),
            pltpu.SemaphoreType.DMA((18,)),
        ],
        out_specs=[ANY] * 2, vmem=56,
    )(self_one, neigh_one, x, history, bias, jnp.transpose(send_rows, (2, 0, 1)))
    sent = [
        lax.ppermute(pack, "cache", [(i, (i + d) % N_CACHE) for i in range(N_CACHE)]) for d in (1, 2, 3)
    ]
    halo = lax.cond(
        me[0] < N_CACHE,
        lambda v: lax.all_to_all(v, "dom", **spread),
        jnp.zeros_like,
        outbound.reshape(dests, SLOT // 4, 4, width),
    )
    halo = halo.reshape(dests * SLOT, width)

    full = call(
        agg_kernel, shape((N_CACHE, rows, width), bf16), [SMEM] * 2 + [VMEM] * 3,
        [
            pltpu.VMEM((HBLK * BLK, width), f32),
            pltpu.VMEM((rows, width), bf16),
            pltpu.SemaphoreType.DMA((LB, N_CACHE)),
        ], out_specs=ANY, flops=10**6
    )(tile_dst, tile_src, mats, x, halo)
    full = lax.all_to_all(full, "cache", **spread)

    side = call(
        side_kernel, shape((2 * N_CACHE + 3, rows + 16, width), bf16),
        [SMEM] * 3 + [VMEM] * 4 + [ANY] * 4,
        [
            pltpu.VMEM((rows, N_CACHE * width), bf16),
            pltpu.VMEM((HBLK * BLK, width), bf16),
            pltpu.VMEM((rows, width), f32),
            pltpu.VMEM((N_CACHE, length, width), bf16),
            pltpu.VMEM((2 * N_CACHE + 3, rows + 16, width), bf16),
            pltpu.SemaphoreType.DMA((N_CACHE, 2)),
        ], out_specs=ANY, flops=10**9, vmem=58,
    )(me, tile_dst, tile_src, mats, self_two, neigh_two, bias_two.reshape(1, -1), pack, *sent)

    return call(
        last_kernel, shape((rows, width), bf16), [SMEM, VMEM, ANY, ANY],
        [
            pltpu.VMEM((LOCAL, BLK, BLK), bf16),
            pltpu.VMEM((2 * N_CACHE + 3, rows + 16, width), bf16),
            pltpu.VMEM((rows, width), f32),
            pltpu.VMEM((rows, width), bf16),
            pltpu.SemaphoreType.DMA((4,)),
        ], vmem=53,
    )(used, full, mats, side)


def solution(mesh):
    return jax.shard_map(
        body,
        mesh=mesh,
        in_specs=(
            P("dom", "cache"),
            P("dom"),
            P("dom", None, None),
            P("dom", None),
            P("dom", None),
            P("dom", None, None, None),
            P(("dom", "cache"), None),
            P(None, "cache"),
            P(None, "cache"),
            P("cache"),
            P(None, "cache"),
            P(None, "cache"),
            P("cache"),
        ),
        out_specs=P("dom", "cache"),
        check_vma=False,
    )
```
